32 devices in a mesh: box: 16 (over z, y, core), src: 2 (over x).
Axes of the slice: x: 2, y: 2, z: 4, core: 2. Of those that a mesh axis runs over, the one named last changes fastest.
Arguments:
- incident: bfloat16 [128, 256, 256], P('box', 'src'), may hold values from -6 to 6
- reflectivity: float32 [128, 128], P('box'), may hold values from 0.5 to 2
- w_self: bfloat16 [3, 128, 2, 128, 128], P(None, 'box'), may hold values from -0.25 to 0.25
- w_cross: bfloat16 [3, 128, 2, 128, 128], P(None, 'box'), may hold values from -0.25 to 0.25
- receivers: int32 [128], P('box'), may hold values from 0 to 127, as said below
- observed: bfloat16 [128, 256, 256], P('box', 'src'), may hold values from -6 to 6
- group_of: int32 [256], P('src'), may hold values from 0 to 15
- deltas: float32 [16], replicated, may hold values from 0.5 to 4
Outputs:
- image_grad: float32 [128, 128], P('box', 'src')
The draws below stay inside these ranges and needn't reach their ends.
Inputs may be any that keep to these rules, and one draw needn't show every extreme that they name: `receivers`: trace t lies in box block t // 8, that is between (8 * (t // 8)) and (8 * (t // 8) + 7).
All inputs are finite; a program needn't handle non-finite values.
Results may differ from the reference program's by a relative error of at most 0.001.
Values may be sent and summed in bfloat16 or wider, within the bound.
A program may use at most 64 MiB of HBM per device.

```python
import math
import jax
import jax.numpy as jnp
from jax import lax

NODES = 128
BOX_DEV = 8
SECTIONS = 3
TRACES = 8
NGROUPS = 16
NB = 128
SOURCES = 256
NT = 128
N_BOX = 16


def draw_receivers(key, part):
    positions = jnp.arange(NT, dtype=jnp.int32)
    block_base = positions // TRACES * BOX_DEV
    offsets = jax.random.randint(key, (NT,), 0, BOX_DEV, dtype=jnp.int32)
    trace_slot = positions % TRACES
    offsets = jnp.where(trace_slot == 0, BOX_DEV - 1, jnp.where(trace_slot == 1, 0, offsets))
    return (block_base + offsets).astype(jnp.int32)


def with_ends(drawn, rng, smallest, largest):
    extent = drawn.shape
    spot = [jax.random.randint(jax.random.fold_in(rng, axis), (), 0, extent[axis]) for axis in range(len(extent))]
    drawn = drawn.at[tuple(spot)].set(smallest)
    longest = extent.index(max(extent))
    spot[longest] = (spot[longest] + 1) % extent[longest]
    return drawn.at[tuple(spot)].set(largest)


def block_levels(own_key, extent, cuts, low, largest):
    gain = 1.0
    for dim, blocks in cuts:
        steps = jax.random.uniform(jax.random.fold_in(jax.random.fold_in(own_key, 6), dim), (blocks,), jnp.float32, low / len(cuts), largest / len(cuts))
        gain = gain * jnp.repeat(jnp.exp(steps), extent[dim] // blocks).reshape((-1,) + (1,) * (len(extent) - 1 - dim))
    return gain


def scatter_about(stream_key, extent, spread, most, pieces=(), held_as=jnp.bfloat16):
    result = spread * jax.random.normal(stream_key, extent, jnp.float32)
    if pieces:
        result = result * block_levels(stream_key, extent, pieces, -0.22, 0.18)
    return jnp.clip(result, -most, most).astype(held_as)


def setup_inputs(seed: int = 0) -> dict:
    key_list = jax.random.split(jax.random.key(seed), 9)
    return {
        "incident": scatter_about(key_list[0], (NB, SOURCES, 2 * NODES), 1.0, 6.0, ((0, 16), (1, 2))),
        "reflectivity": jnp.clip(jnp.exp(math.log(2.0) - 1.3862944 * jax.random.uniform(key_list[1], (NB, NODES), jnp.float32) ** block_levels(key_list[1], (NB, NODES), ((0, 16),), -0.2, 0.2)), 0.5, 2.0),
        "w_self": scatter_about(key_list[2], (SECTIONS, NB, 2, NODES, NODES), (4 * NODES) ** -0.5, 0.25, ((1, 16),)),
        "w_cross": scatter_about(key_list[3], (SECTIONS, NB, 2, NODES, NODES), (4 * NODES) ** -0.5, 0.25, ((1, 16),)),
        "receivers": draw_receivers(jax.random.fold_in(key_list[8], 71), 0),
        "observed": scatter_about(key_list[5], (NT, SOURCES, 2 * NODES), 1.0, 6.0, ((0, 16), (1, 2))),
        "group_of": with_ends(jax.random.randint(key_list[6], (SOURCES,), 0, NGROUPS), jax.random.fold_in(key_list[6], 1), 0, NGROUPS - 1).astype(jnp.int32),
        "deltas": jnp.clip(jnp.exp(jax.random.uniform(key_list[7], (NGROUPS,), jnp.float32, math.log(0.5), math.log(4.0))), 0.5, 4.0),
    }


def block_form(weights):
    real_part = weights[:, 0].astype(jnp.float32)
    imag_part = weights[:, 1].astype(jnp.float32)
    upper_rows = jnp.concatenate([real_part, imag_part], axis=2)
    lower_rows = jnp.concatenate([-imag_part, real_part], axis=2)
    return jnp.concatenate([upper_rows, lower_rows], axis=1)

def partner_of(values, swap_bit):
    blocks = values.reshape((N_BOX, BOX_DEV) + values.shape[1:])
    order = (jnp.arange(N_BOX, dtype=jnp.int32) ^ 1 << swap_bit).astype(jnp.int32)
    return blocks[order].reshape(values.shape)

def forward_apply(values, block):
    return jnp.einsum('bsi,bij->bsj', values.astype(jnp.float32), block)

def adjoint_apply(values, block):
    return jnp.einsum('bsj,bij->bsi', values.astype(jnp.float32), block)

def reference(incident, reflectivity, w_self, w_cross, receivers, observed, group_of, deltas):
    top_bit = N_BOX.bit_length() - 1
    doubled = jnp.concatenate([reflectivity, reflectivity], axis=1)
    wavefield = (doubled[:, None, :] * incident.astype(jnp.float32)).astype(jnp.bfloat16)
    for section_idx in range(SECTIONS):
        swap_bit = top_bit - 1 - section_idx
        partner_field = partner_of(wavefield, swap_bit)
        summed = forward_apply(wavefield, block_form(w_self[section_idx])) + forward_apply(partner_field, block_form(w_cross[section_idx]))
        wavefield = summed.astype(jnp.bfloat16)
    predicted = wavefield[receivers].astype(jnp.float32)
    residual = predicted - observed.astype(jnp.float32)
    magnitude = residual[..., :NODES] ** 2 + residual[..., NODES:] ** 2
    scale_src = deltas[group_of]
    damping = 1.0 / jnp.sqrt(1.0 + magnitude / scale_src[None, :, None] ** 2)
    adj_traces = (residual * jnp.concatenate([damping, damping], axis=2)).astype(jnp.bfloat16)
    adjoint_field = jax.ops.segment_sum(adj_traces.astype(jnp.float32), receivers, num_segments=NB).astype(jnp.bfloat16)
    for section_idx in reversed(range(SECTIONS)):
        swap_bit = top_bit - 1 - section_idx
        outgoing = adjoint_apply(adjoint_field, block_form(w_cross[section_idx])).astype(jnp.bfloat16)
        received = partner_of(outgoing, swap_bit)
        summed = adjoint_apply(adjoint_field, block_form(w_self[section_idx])) + received.astype(jnp.float32)
        adjoint_field = summed.astype(jnp.bfloat16)
    products = incident.astype(jnp.float32) * adjoint_field.astype(jnp.float32)
    return lax.optimization_barrier(jnp.sum(products[..., :NODES] + products[..., NODES:], axis=1))
```

```python
import functools

import jax
import jax.numpy as jnp
from jax import lax
from jax.experimental import pallas as pl
from jax.experimental.pallas import tpu as pltpu
from jax.sharding import PartitionSpec as P

PARTS = 2
GROUP = 1
LAG = 1
AHEAD = 16
MESH = pl.DeviceIdType.MESH


def rows_by_cols(values, block):
    return lax.dot_general(values, block, (((1,), (0,)), ((), ())), preferred_element_type=jnp.float32)


def rows_by_rows(values, block):
    return lax.dot_general(values, block, (((1,), (1,)), ((), ())), preferred_element_type=jnp.float32)


def kernel(n_box, n_src, inc_hbm, refl_hbm, ws_hbm, wc_hbm, recv_ref, obs_hbm, group_ref, deltas_ref, out_ref,
           inc, pinc, refl, prefl, ws, wc, obs, bs, bc, field, got, inv2, grads, top, cross, back,
           image, image_cross, arrived, local_sem, send_sem, recv_sem, refl_sem, fin_send, fin_recv):
    boxes, sources, width = inc.shape
    nodes = width // 2
    sections = ws.shape[0]
    rows = sources // PARTS
    per_part = boxes // GROUP
    units = PARTS * per_part
    me_box = lax.axis_index("box")
    me_src = lax.axis_index("src")

    def partner(section):
        stride = n_box >> (section + 1)
        return me_box + stride * (1 - 2 * ((me_box // stride) % 2))

    far = partner(0)

    local = [
        pltpu.make_async_copy(ws_hbm, ws, local_sem.at[0]),
        pltpu.make_async_copy(wc_hbm, wc, local_sem.at[1]),
        pltpu.make_async_copy(inc_hbm, inc, local_sem.at[2]),
        pltpu.make_async_copy(refl_hbm, refl, local_sem.at[3]),
        pltpu.make_async_copy(obs_hbm, obs, local_sem.at[4]),
    ]
    for copy in local:
        copy.start()

    barrier = pltpu.get_barrier_semaphore()
    others = [(partner(s), me_src) for s in range(sections)]
    for step in range(1, n_src):
        others.append((me_box, (me_src + step) % n_src))
        others.append((far, (me_src + step) % n_src))
    for other in others:
        pl.semaphore_signal(barrier, inc=1, device_id=other, device_id_type=MESH)
    pl.semaphore_wait(barrier, len(others))

    def place(unit):
        part = unit // per_part
        return pl.multiple_of((unit - part * per_part) * GROUP, GROUP), pl.multiple_of(part * rows, rows)

    def remote(kind, unit):
        box0, row0 = place(unit)
        where = (pl.ds(box0, GROUP), pl.ds(row0, rows))
        if kind == 0:
            source, target, section = inc_hbm.at[where], pinc.at[where], 0
        elif kind < sections:
            source, target, section = field.at[(kind - 1,) + where], got.at[(kind - 1,) + where], kind
        else:
            section = kind - sections + 1
            source, target = cross.at[(section - 1,) + where], back.at[(section - 1,) + where]
        return pltpu.make_async_remote_copy(
            src_ref=source, dst_ref=target, send_sem=send_sem.at[kind, unit], recv_sem=recv_sem.at[kind, unit],
            device_id=(partner(section), me_src), device_id_type=MESH)

    refl_copy = pltpu.make_async_remote_copy(
        src_ref=refl_hbm, dst_ref=prefl, send_sem=refl_sem.at[0], recv_sem=refl_sem.at[1],
        device_id=(far, me_src), device_id_type=MESH)
    refl_copy.start()

    @pl.loop(0, min(AHEAD, units))
    def _(unit):
        remote(0, unit).start()

    scale = jnp.zeros((1, sources), jnp.float32)
    groups = group_ref[...].reshape(1, sources)
    for k in range(deltas_ref.shape[0]):
        scale = jnp.where(groups == k, deltas_ref[k], scale)
    inv2[...] = jnp.broadcast_to(1.0 / (scale * scale), (nodes, sources)).T
    image[...] = jnp.zeros_like(image)
    image_cross[...] = jnp.zeros_like(image_cross)

    for copy in local:
        copy.wait()
    for section in range(sections):
        @pl.loop(0, boxes)
        def _(box):
            for raw, block in ((ws, bs), (wc, bc)):
                real = raw[section, box, 0]
                imag = raw[section, box, 1]
                block[section, box, :nodes, :nodes] = real
                block[section, box, :nodes, nodes:] = imag
                block[section, box, nodes:, :nodes] = -imag
                block[section, box, nodes:, nodes:] = real
    refl_copy.wait_recv()

    def each_box(unit, work):
        box0, row0 = place(unit)
        for i in range(GROUP):
            work(box0 + i, pl.ds(row0, rows))

    def forward(section, unit):
        remote(section, unit).wait_recv()

        def work(box, span):
            if section == 0:
                one = refl[pl.ds(box, 1), :]
                two = prefl[pl.ds(box, 1), :]
                own = (jnp.concatenate([one, one], axis=1) * inc[box, span, :].astype(jnp.float32)).astype(jnp.bfloat16)
                other = (jnp.concatenate([two, two], axis=1) * pinc[box, span, :].astype(jnp.float32)).astype(jnp.bfloat16)
            else:
                own = field[section - 1, box, span, :]
                other = got[section - 1, box, span, :]
            summed = rows_by_cols(own, bs[section, box]) + rows_by_cols(other, bc[section, box])
            field[section, box, span, :] = summed.astype(jnp.bfloat16)

        each_box(unit, work)
        if section < sections - 1:
            remote(section + 1, unit).start()

    def traces(part):
        span = pl.ds(pl.multiple_of(part * rows, rows), rows)

        @pl.loop(0, recv_ref.shape[0])
        def _(t):
            residual = field[sections - 1, lax.rem(recv_ref[t], boxes), span, :].astype(jnp.float32) - obs[t, span, :].astype(jnp.float32)
            magnitude = residual[:, :nodes] ** 2 + residual[:, nodes:] ** 2
            damping = 1.0 / jnp.sqrt(1.0 + magnitude * inv2[span, :])
            grads[t] = (residual * jnp.concatenate([damping, damping], axis=1)).astype(jnp.bfloat16)

        def adjoint_unit(unit):
            def work(box, span):
                total = jnp.zeros((rows, width), jnp.float32)
                for t in range(recv_ref.shape[0]):
                    hit = jnp.where(lax.rem(recv_ref[t], boxes) == box, 1.0, 0.0)
                    total += grads[t].astype(jnp.float32) * hit
                value = total.astype(jnp.bfloat16)
                top[sections - 1, box, span, :] = value
                cross[sections - 2, box, span, :] = rows_by_rows(value, bc[sections - 1, box]).astype(jnp.bfloat16)

            each_box(unit, work)
            remote(2 * sections - 2, unit).start()

        @pl.loop(0, per_part)
        def _(i):
            adjoint_unit(part * per_part + i)

    def adjoint(section, unit):
        remote(sections + section - 1, unit).wait_recv()

        def work(box, span):
            below = rows_by_rows(top[section, box, span, :], bs[section, box]) + back[section - 1, box, span, :].astype(jnp.float32)
            value = below.astype(jnp.bfloat16)
            other = rows_by_rows(value, bc[section - 1, box])
            if section > 1:
                top[section - 1, box, span, :] = value
                cross[section - 2, box, span, :] = other.astype(jnp.bfloat16)
            else:
                own = rows_by_rows(value, bs[0, box])
                for result, term, wave in ((image, own, inc), (image_cross, other, pinc)):
                    product = term * wave[box, span, :].astype(jnp.float32)
                    result[pl.ds(box, 1), :] += jnp.sum(product[:, :nodes] + product[:, nodes:], axis=0, keepdims=True)

        each_box(unit, work)
        if section > 1:
            remote(sections + section - 2, unit).start()

    last = (sections - 1) * LAG
    turn = per_part + last
    steps = units + turn + (sections - 2) * LAG

    @pl.loop(0, steps)
    def _(step):
        if AHEAD < units:
            @pl.when(step + AHEAD < units)
            def _():
                remote(0, step + AHEAD).start()
        for section in range(sections):
            unit = step - section * LAG

            @pl.when((unit >= 0) & (unit < units))
            def _():
                forward(section, unit)
        done = step - last + 1
        part = done // per_part

        @pl.when((done > 0) & (done <= units) & (done == part * per_part))
        def _():
            traces(part - 1)
        for section in range(sections - 1, 0, -1):
            unit = step - turn - (sections - 1 - section) * LAG

            @pl.when((unit >= 0) & (unit < units))
            def _():
                adjoint(section, unit)

    final = []
    for step in range(n_src):
        if step:
            final.append(pltpu.make_async_remote_copy(
                src_ref=image, dst_ref=arrived.at[0, step], send_sem=fin_send.at[0, step], recv_sem=fin_recv.at[0, step],
                device_id=(me_box, (me_src + step) % n_src), device_id_type=MESH))
        final.append(pltpu.make_async_remote_copy(
            src_ref=image_cross, dst_ref=arrived.at[1, step], send_sem=fin_send.at[1, step], recv_sem=fin_recv.at[1, step],
            device_id=(far, (me_src + step) % n_src), device_id_type=MESH))
    for copy in final:
        copy.start()

    refl_copy.wait_send()

    @pl.loop(0, units)
    def _(unit):
        for kind in range(2 * sections - 1):
            remote(kind, unit).wait_send()

    for copy in final:
        copy.wait()
    total = image[...] + arrived[1, 0]
    for step in range(1, n_src):
        total += arrived[0, step] + arrived[1, step]
    share = nodes // n_src
    for k in range(n_src):
        @pl.when(me_src == k)
        def _():
            out_ref[...] = total[:, k * share:(k + 1) * share]


def body(n_box, n_src, incident, reflectivity, w_self, w_cross, receivers, observed, group_of, deltas):
    boxes, sources, width = incident.shape
    nodes = width // 2
    sections = w_self.shape[0]
    units = PARTS * (boxes // GROUP)
    wave = (boxes, sources, width)
    anywhere = pl.BlockSpec(memory_space=pl.ANY)
    scalars = pl.BlockSpec(memory_space=pltpu.SMEM)
    vector = pl.BlockSpec(memory_space=pltpu.VMEM)
    bf16, f32 = jnp.bfloat16, jnp.float32
    return pl.pallas_call(
        functools.partial(kernel, n_box, n_src),
        out_shape=jax.ShapeDtypeStruct((boxes, nodes // n_src), f32),
        in_specs=[anywhere, anywhere, anywhere, anywhere, scalars, anywhere, vector, scalars],
        out_specs=vector,
        scratch_shapes=[
            pltpu.VMEM(wave, bf16),
            pltpu.VMEM(wave, bf16),
            pltpu.VMEM((boxes, nodes), f32),
            pltpu.VMEM((boxes, nodes), f32),
            pltpu.VMEM(w_self.shape, bf16),
            pltpu.VMEM(w_cross.shape, bf16),
            pltpu.VMEM(observed.shape, bf16),
            pltpu.VMEM((sections, boxes, width, width), bf16),
            pltpu.VMEM((sections, boxes, width, width), bf16),
            pltpu.VMEM((sections,) + wave, bf16),
            pltpu.VMEM((sections - 1,) + wave, bf16),
            pltpu.VMEM((sources, nodes), f32),
            pltpu.VMEM((receivers.shape[0], sources // PARTS, width), bf16),
            pltpu.VMEM((sections,) + wave, bf16),
            pltpu.VMEM((sections - 1,) + wave, bf16),
            pltpu.VMEM((sections - 1,) + wave, bf16),
            pltpu.VMEM((boxes, nodes), f32),
            pltpu.VMEM((boxes, nodes), f32),
            pltpu.VMEM((2, n_src, boxes, nodes), f32),
            pltpu.SemaphoreType.DMA((5,)),
            pltpu.SemaphoreType.DMA((2 * sections - 1, units)),
            pltpu.SemaphoreType.DMA((2 * sections - 1, units)),
            pltpu.SemaphoreType.DMA((2,)),
            pltpu.SemaphoreType.DMA((2, n_src)),
            pltpu.SemaphoreType.DMA((2, n_src)),
        ],
        compiler_params=pltpu.CompilerParams(
            collective_id=0, has_side_effects=True, vmem_limit_bytes=56 * 1024 * 1024),
    )(incident, reflectivity, w_self, w_cross, receivers, observed, group_of, deltas)


def solution(mesh):
    in_specs = (
        P("box", "src", None),
        P("box", None),
        P(None, "box", None, None, None),
        P(None, "box", None, None, None),
        P("box"),
        P("box", "src", None),
        P("src"),
        P(),
    )
    run = functools.partial(body, mesh.shape["box"], mesh.shape["src"])
    return jax.shard_map(run, mesh=mesh, in_specs=in_specs, out_specs=P("box", "src"), check_vma=False)
```

```python
import functools

import jax
import jax.numpy as jnp
from jax import lax
from jax.experimental import pallas as pl
from jax.experimental.pallas import tpu as pltpu
from jax.sharding import PartitionSpec as P

PARTS = 4
GROUP = 4
LAG = 2
AHEAD = 2
MESH = pl.DeviceIdType.MESH


def rows_by_cols(values, block):
    return lax.dot_general(values, block, (((1,), (0,)), ((), ())), preferred_element_type=jnp.float32)


def kernel(n_box, n_src, inc_hbm, refl_hbm, ws_hbm, wc_hbm, recv_ref, obs_hbm, group_ref, deltas_ref, out_ref,
           inc, pinc, refl, prefl, ws, wc, obs, bs, bc, bst, bct, field, got, inv2, grads, top, cross, back,
           image, image_cross, arrived, local_sem, send_sem, recv_sem, refl_sem, fin_send, fin_recv):
    boxes, sources, width = inc.shape
    nodes = width // 2
    sections = ws.shape[0]
    rows = sources // PARTS
    per_part = boxes // GROUP
    units = PARTS * per_part
    me_box = lax.axis_index("box")
    me_src = lax.axis_index("src")

    def partner(section):
        stride = n_box >> (section + 1)
        return me_box + stride * (1 - 2 * ((me_box // stride) % 2))

    far = partner(0)

    local = [
        pltpu.make_async_copy(ws_hbm, ws, local_sem.at[0]),
        pltpu.make_async_copy(wc_hbm, wc, local_sem.at[1]),
        pltpu.make_async_copy(inc_hbm, inc, local_sem.at[2]),
        pltpu.make_async_copy(refl_hbm, refl, local_sem.at[3]),
        pltpu.make_async_copy(obs_hbm, obs, local_sem.at[4]),
    ]
    for copy in local:
        copy.start()

    barrier = pltpu.get_barrier_semaphore()
    others = [(partner(s), me_src) for s in range(sections)]
    for step in range(1, n_src):
        others.append((me_box, (me_src + step) % n_src))
        others.append((far, (me_src + step) % n_src))
    for other in others:
        pl.semaphore_signal(barrier, inc=1, device_id=other, device_id_type=MESH)
    pl.semaphore_wait(barrier, len(others))

    def place(unit):
        part = unit // per_part
        return pl.multiple_of((unit - part * per_part) * GROUP, GROUP), pl.multiple_of(part * rows, rows)

    def remote(kind, unit):
        box0, row0 = place(unit)
        where = (pl.ds(box0, GROUP), pl.ds(row0, rows))
        if kind == 0:
            source, target, section = inc_hbm.at[where], pinc.at[where], 0
        elif kind < sections:
            source, target, section = field.at[(kind - 1,) + where], got.at[(kind - 1,) + where], kind
        else:
            section = kind - sections + 1
            source, target = cross.at[(section - 1,) + where], back.at[(section - 1,) + where]
        return pltpu.make_async_remote_copy(
            src_ref=source, dst_ref=target, send_sem=send_sem.at[kind, unit], recv_sem=recv_sem.at[kind, unit],
            device_id=(partner(section), me_src), device_id_type=MESH)

    refl_copy = pltpu.make_async_remote_copy(
        src_ref=refl_hbm, dst_ref=prefl, send_sem=refl_sem.at[0], recv_sem=refl_sem.at[1],
        device_id=(far, me_src), device_id_type=MESH)
    refl_copy.start()

    @pl.loop(0, min(AHEAD, units))
    def _(unit):
        remote(0, unit).start()

    scale = jnp.zeros((1, sources), jnp.float32)
    groups = group_ref[...].reshape(1, sources)
    for k in range(deltas_ref.shape[0]):
        scale = jnp.where(groups == k, deltas_ref[k], scale)
    inv2[...] = jnp.broadcast_to(1.0 / (scale * scale), (nodes, sources)).T
    image[...] = jnp.zeros_like(image)
    image_cross[...] = jnp.zeros_like(image_cross)

    for copy in local:
        copy.wait()
    for section in range(sections):
        @pl.loop(0, boxes)
        def _(box):
            for raw, block in ((ws, bs), (wc, bc)):
                real = raw[section, box, 0]
                imag = raw[section, box, 1]
                block[section, box, :nodes, :nodes] = real
                block[section, box, :nodes, nodes:] = imag
                block[section, box, nodes:, :nodes] = -imag
                block[section, box, nodes:, nodes:] = real
    refl_copy.wait_recv()

    def transpose_blocks(box):
        @pl.loop(0, sections)
        def _(section):
            for raw, block in ((ws, bst), (wc, bct)):
                real = raw[section, box, 0].T
                imag = raw[section, box, 1].T
                block[section, box, :nodes, :nodes] = real
                block[section, box, :nodes, nodes:] = -imag
                block[section, box, nodes:, :nodes] = imag
                block[section, box, nodes:, nodes:] = real

    def each_box(unit, work):
        box0, row0 = place(unit)
        for i in range(GROUP):
            work(box0 + i, pl.ds(row0, rows))

    def forward(section, unit):
        remote(section, unit).wait_recv()

        def work(box, span):
            if section == 0:
                one = refl[pl.ds(box, 1), :]
                two = prefl[pl.ds(box, 1), :]
                own = (jnp.concatenate([one, one], axis=1) * inc[box, span, :].astype(jnp.float32)).astype(jnp.bfloat16)
                other = (jnp.concatenate([two, two], axis=1) * pinc[box, span, :].astype(jnp.float32)).astype(jnp.bfloat16)
            else:
                own = field[section - 1, box, span, :]
                other = got[section - 1, box, span, :]
            summed = rows_by_cols(own, bs[section, box]) + rows_by_cols(other, bc[section, box])
            field[section, box, span, :] = summed.astype(jnp.bfloat16)

        each_box(unit, work)
        if section < sections - 1:
            remote(section + 1, unit).start()

    def traces(part):
        span = pl.ds(pl.multiple_of(part * rows, rows), rows)

        @pl.loop(0, recv_ref.shape[0])
        def _(t):
            residual = field[sections - 1, lax.rem(recv_ref[t], boxes), span, :].astype(jnp.float32) - obs[t, span, :].astype(jnp.float32)
            magnitude = residual[:, :nodes] ** 2 + residual[:, nodes:] ** 2
            damping = 1.0 / jnp.sqrt(1.0 + magnitude * inv2[span, :])
            grads[t] = (residual * jnp.concatenate([damping, damping], axis=1)).astype(jnp.bfloat16)

        def adjoint_unit(unit):
            def work(box, span):
                total = jnp.zeros((rows, width), jnp.float32)
                for t in range(recv_ref.shape[0]):
                    hit = jnp.where(lax.rem(recv_ref[t], boxes) == box, 1.0, 0.0)
                    total += grads[t].astype(jnp.float32) * hit
                value = total.astype(jnp.bfloat16)
                top[sections - 1, box, span, :] = value
                cross[sections - 2, box, span, :] = rows_by_cols(value, bct[sections - 1, box]).astype(jnp.bfloat16)

            each_box(unit, work)
            remote(2 * sections - 2, unit).start()

        @pl.loop(0, per_part)
        def _(i):
            adjoint_unit(part * per_part + i)

    def adjoint(section, unit):
        remote(sections + section - 1, unit).wait_recv()

        def work(box, span):
            below = rows_by_cols(top[section, box, span, :], bst[section, box]) + back[section - 1, box, span, :].astype(jnp.float32)
            value = below.astype(jnp.bfloat16)
            other = rows_by_cols(value, bct[section - 1, box])
            if section > 1:
                top[section - 1, box, span, :] = value
                cross[section - 2, box, span, :] = other.astype(jnp.bfloat16)
            else:
                own = rows_by_cols(value, bst[0, box])
                for result, term, wave in ((image, own, inc), (image_cross, other, pinc)):
                    product = term * wave[box, span, :].astype(jnp.float32)
                    result[pl.ds(box, 1), :] += jnp.sum(product[:, :nodes] + product[:, nodes:], axis=0, keepdims=True)

        each_box(unit, work)
        if section > 1:
            remote(sections + section - 2, unit).start()

    last = (sections - 1) * LAG
    turn = per_part + last
    per_step = -(-boxes // turn)
    steps = units + turn + (sections - 2) * LAG

    @pl.loop(0, steps)
    def _(step):
        if AHEAD < units:
            @pl.when(step + AHEAD < units)
            def _():
                remote(0, step + AHEAD).start()
        for section in range(sections):
            unit = step - section * LAG

            @pl.when((unit >= 0) & (unit < units))
            def _():
                forward(section, unit)
        for i in range(per_step):
            @pl.when(step * per_step + i < boxes)
            def _():
                transpose_blocks(step * per_step + i)
        done = step - last + 1
        part = done // per_part

        @pl.when((done > 0) & (done <= units) & (done == part * per_part))
        def _():
            traces(part - 1)
        for section in range(sections - 1, 0, -1):
            unit = step - turn - (sections - 1 - section) * LAG

            @pl.when((unit >= 0) & (unit < units))
            def _():
                adjoint(section, unit)

    final = []
    for step in range(n_src):
        if step:
            final.append(pltpu.make_async_remote_copy(
                src_ref=image, dst_ref=arrived.at[0, step], send_sem=fin_send.at[0, step], recv_sem=fin_recv.at[0, step],
                device_id=(me_box, (me_src + step) % n_src), device_id_type=MESH))
        final.append(pltpu.make_async_remote_copy(
            src_ref=image_cross, dst_ref=arrived.at[1, step], send_sem=fin_send.at[1, step], recv_sem=fin_recv.at[1, step],
            device_id=(far, (me_src + step) % n_src), device_id_type=MESH))
    for copy in final:
        copy.start()

    refl_copy.wait_send()

    @pl.loop(0, units)
    def _(unit):
        for kind in range(2 * sections - 1):
            remote(kind, unit).wait_send()

    for copy in final:
        copy.wait()
    total = image[...] + arrived[1, 0]
    for step in range(1, n_src):
        total += arrived[0, step] + arrived[1, step]
    share = nodes // n_src
    for k in range(n_src):
        @pl.when(me_src == k)
        def _():
            out_ref[...] = total[:, k * share:(k + 1) * share]


def body(n_box, n_src, incident, reflectivity, w_self, w_cross, receivers, observed, group_of, deltas):
    boxes, sources, width = incident.shape
    nodes = width // 2
    sections = w_self.shape[0]
    units = PARTS * (boxes // GROUP)
    wave = (boxes, sources, width)
    anywhere = pl.BlockSpec(memory_space=pl.ANY)
    scalars = pl.BlockSpec(memory_space=pltpu.SMEM)
    vector = pl.BlockSpec(memory_space=pltpu.VMEM)
    bf16, f32 = jnp.bfloat16, jnp.float32
    return pl.pallas_call(
        functools.partial(kernel, n_box, n_src),
        out_shape=jax.ShapeDtypeStruct((boxes, nodes // n_src), f32),
        in_specs=[anywhere, anywhere, anywhere, anywhere, scalars, anywhere, vector, scalars],
        out_specs=vector,
        scratch_shapes=[
            pltpu.VMEM(wave, bf16),
            pltpu.VMEM(wave, bf16),
            pltpu.VMEM((boxes, nodes), f32),
            pltpu.VMEM((boxes, nodes), f32),
            pltpu.VMEM(w_self.shape, bf16),
            pltpu.VMEM(w_cross.shape, bf16),
            pltpu.VMEM(observed.shape, bf16),
            pltpu.VMEM((sections, boxes, width, width), bf16),
            pltpu.VMEM((sections, boxes, width, width), bf16),
            pltpu.VMEM((sections, boxes, width, width), bf16),
            pltpu.VMEM((sections, boxes, width, width), bf16),
            pltpu.VMEM((sections,) + wave, bf16),
            pltpu.VMEM((sections - 1,) + wave, bf16),
            pltpu.VMEM((sources, nodes), f32),
            pltpu.VMEM((receivers.shape[0], sources // PARTS, width), bf16),
            pltpu.VMEM((sections,) + wave, bf16),
            pltpu.VMEM((sections - 1,) + wave, bf16),
            pltpu.VMEM((sections - 1,) + wave, bf16),
            pltpu.VMEM((boxes, nodes), f32),
            pltpu.VMEM((boxes, nodes), f32),
            pltpu.VMEM((2, n_src, boxes, nodes), f32),
            pltpu.SemaphoreType.DMA((5,)),
            pltpu.SemaphoreType.DMA((2 * sections - 1, units)),
            pltpu.SemaphoreType.DMA((2 * sections - 1, units)),
            pltpu.SemaphoreType.DMA((2,)),
            pltpu.SemaphoreType.DMA((2, n_src)),
            pltpu.SemaphoreType.DMA((2, n_src)),
        ],
        compiler_params=pltpu.CompilerParams(
            collective_id=0, has_side_effects=True, vmem_limit_bytes=56 * 1024 * 1024),
    )(incident, reflectivity, w_self, w_cross, receivers, observed, group_of, deltas)


def solution(mesh):
    in_specs = (
        P("box", "src", None),
        P("box", None),
        P(None, "box", None, None, None),
        P(None, "box", None, None, None),
        P("box"),
        P("box", "src", None),
        P("src"),
        P(),
    )
    run = functools.partial(body, mesh.shape["box"], mesh.shape["src"])
    return jax.shard_map(run, mesh=mesh, in_specs=in_specs, out_specs=P("box", "src"), check_vma=False)
```

```python
import functools

import jax
import jax.numpy as jnp
from jax import lax
from jax.experimental import pallas as pl
from jax.experimental.pallas import tpu as pltpu
from jax.sharding import PartitionSpec as P

PARTS = 4
GROUP = 4
LAG = 2
AHEAD = 2
REST = 1
MESH = pl.DeviceIdType.MESH


def rows_by_cols(values, block):
    return lax.dot_general(values, block, (((1,), (0,)), ((), ())), preferred_element_type=jnp.float32)


def kernel(n_box, n_src, inc_hbm, refl_hbm, ws_hbm, wc_hbm, recv_ref, obs_hbm, group_ref, deltas_ref, out_ref,
           inc, pinc, refl, prefl, ws, wc, obs, bs, bc, bst, bct, field, got, inv2, grads, top, cross, back,
           image, image_cross, arrived, local_sem, send_sem, recv_sem, refl_sem, fin_send, fin_recv):
    boxes, sources, width = inc.shape
    nodes = width // 2
    sections = ws.shape[0]
    rows = sources // PARTS
    per_part = boxes // GROUP
    units = PARTS * per_part
    me_box = lax.axis_index("box")
    me_src = lax.axis_index("src")

    def partner(section):
        stride = n_box >> (section + 1)
        return me_box + stride * (1 - 2 * ((me_box // stride) % 2))

    far = partner(0)

    local = [
        pltpu.make_async_copy(ws_hbm, ws, local_sem.at[0]),
        pltpu.make_async_copy(wc_hbm, wc, local_sem.at[1]),
        pltpu.make_async_copy(inc_hbm, inc, local_sem.at[2]),
        pltpu.make_async_copy(refl_hbm, refl, local_sem.at[3]),
        pltpu.make_async_copy(obs_hbm, obs, local_sem.at[4]),
    ]
    for copy in local:
        copy.start()

    barrier = pltpu.get_barrier_semaphore()
    others = [(partner(s), me_src) for s in range(sections)]
    for step in range(1, n_src):
        others.append((me_box, (me_src + step) % n_src))
        others.append((far, (me_src + step) % n_src))
    for other in others:
        pl.semaphore_signal(barrier, inc=1, device_id=other, device_id_type=MESH)
    pl.semaphore_wait(barrier, len(others))

    def place(unit):
        part = unit // per_part
        return pl.multiple_of((unit - part * per_part) * GROUP, GROUP), pl.multiple_of(part * rows, rows)

    def remote(kind, unit):
        box0, row0 = place(unit)
        where = (pl.ds(box0, GROUP), pl.ds(row0, rows))
        if kind == 0:
            source, target, section = inc_hbm.at[where], pinc.at[where], 0
        elif kind < sections:
            source, target, section = field.at[(kind - 1,) + where], got.at[(kind - 1,) + where], kind
        else:
            section = kind - sections + 1
            source, target = cross.at[(section - 1,) + where], back.at[(section - 1,) + where]
        return pltpu.make_async_remote_copy(
            src_ref=source, dst_ref=target, send_sem=send_sem.at[kind, unit], recv_sem=recv_sem.at[kind, unit],
            device_id=(partner(section), me_src), device_id_type=MESH)

    refl_copy = pltpu.make_async_remote_copy(
        src_ref=refl_hbm, dst_ref=prefl, send_sem=refl_sem.at[0], recv_sem=refl_sem.at[1],
        device_id=(far, me_src), device_id_type=MESH)
    refl_copy.start()

    @pl.loop(0, min(AHEAD, units))
    def _(unit):
        remote(0, unit).start()

    scale = jnp.zeros((1, sources), jnp.float32)
    groups = group_ref[...].reshape(1, sources)
    for k in range(deltas_ref.shape[0]):
        scale = jnp.where(groups == k, deltas_ref[k], scale)
    inv2[...] = jnp.broadcast_to(1.0 / (scale * scale), (nodes, sources)).T
    image[...] = jnp.zeros_like(image)
    image_cross[...] = jnp.zeros_like(image_cross)

    for copy in local:
        copy.wait()
    for section in range(sections):
        @pl.loop(0, boxes)
        def _(box):
            for raw, block in ((ws, bs), (wc, bc)):
                real = raw[section, box, 0]
                imag = raw[section, box, 1]
                block[section, box, :nodes, :nodes] = real
                block[section, box, :nodes, nodes:] = imag
                block[section, box, nodes:, :nodes] = -imag
                block[section, box, nodes:, nodes:] = real
    refl_copy.wait_recv()

    def transpose_blocks(box):
        @pl.loop(0, sections)
        def _(section):
            for raw, block in ((ws, bst), (wc, bct)):
                real = raw[section, box, 0].T
                imag = raw[section, box, 1].T
                block[section, box, :nodes, :nodes] = real
                block[section, box, :nodes, nodes:] = -imag
                block[section, box, nodes:, :nodes] = imag
                block[section, box, nodes:, nodes:] = real

    def each_box(unit, work, keep):
        box0, row0 = place(unit)
        span = pl.ds(row0, rows)
        results = [work(box0 + i, span) for i in range(GROUP)]
        for i in range(GROUP):
            keep(box0 + i, span, *results[i])

    def forward(section, unit):
        remote(section, unit).wait_recv()

        def work(box, span):
            if section == 0:
                one = refl[pl.ds(box, 1), :]
                two = prefl[pl.ds(box, 1), :]
                own = (jnp.concatenate([one, one], axis=1) * inc[box, span, :].astype(jnp.float32)).astype(jnp.bfloat16)
                other = (jnp.concatenate([two, two], axis=1) * pinc[box, span, :].astype(jnp.float32)).astype(jnp.bfloat16)
            else:
                own = field[section - 1, box, span, :]
                other = got[section - 1, box, span, :]
            summed = rows_by_cols(own, bs[section, box]) + rows_by_cols(other, bc[section, box])
            return (summed.astype(jnp.bfloat16),)

        def keep(box, span, value):
            field[section, box, span, :] = value

        each_box(unit, work, keep)
        if section < sections - 1:
            remote(section + 1, unit).start()

    def traces(part):
        span = pl.ds(pl.multiple_of(part * rows, rows), rows)

        @pl.loop(0, recv_ref.shape[0])
        def _(t):
            residual = field[sections - 1, lax.rem(recv_ref[t], boxes), span, :].astype(jnp.float32) - obs[t, span, :].astype(jnp.float32)
            magnitude = residual[:, :nodes] ** 2 + residual[:, nodes:] ** 2
            damping = 1.0 / jnp.sqrt(1.0 + magnitude * inv2[span, :])
            grads[t] = (residual * jnp.concatenate([damping, damping], axis=1)).astype(jnp.bfloat16)

        def adjoint_unit(unit):
            def work(box, span):
                total = jnp.zeros((rows, width), jnp.float32)
                for t in range(recv_ref.shape[0]):
                    hit = jnp.where(lax.rem(recv_ref[t], boxes) == box, 1.0, 0.0)
                    total += grads[t].astype(jnp.float32) * hit
                value = total.astype(jnp.bfloat16)
                return value, rows_by_cols(value, bct[sections - 1, box]).astype(jnp.bfloat16)

            def keep(box, span, value, other):
                top[sections - 1, box, span, :] = value
                cross[sections - 2, box, span, :] = other

            each_box(unit, work, keep)
            remote(2 * sections - 2, unit).start()

        @pl.loop(0, per_part)
        def _(i):
            adjoint_unit(part * per_part + i)

    def adjoint(section, unit):
        remote(sections + section - 1, unit).wait_recv()

        def work(box, span):
            below = rows_by_cols(top[section, box, span, :], bst[section, box]) + back[section - 1, box, span, :].astype(jnp.float32)
            value = below.astype(jnp.bfloat16)
            other = rows_by_cols(value, bct[section - 1, box])
            if section > 1:
                return value, other.astype(jnp.bfloat16)
            own = rows_by_cols(value, bst[0, box])
            sums = []
            for term, wave in ((own, inc), (other, pinc)):
                product = term * wave[box, span, :].astype(jnp.float32)
                sums.append(jnp.sum(product[:, :nodes] + product[:, nodes:], axis=0, keepdims=True))
            return sums

        def keep(box, span, first, second):
            if section > 1:
                top[section - 1, box, span, :] = first
                cross[section - 2, box, span, :] = second
            else:
                image[pl.ds(box, 1), :] += first
                image_cross[pl.ds(box, 1), :] += second

        each_box(unit, work, keep)
        if section > 1:
            remote(sections + section - 2, unit).start()

    last = (sections - 1) * LAG
    turn = per_part + last + REST
    per_step = -(-boxes // (per_part + last))
    steps = units + turn + (sections - 2) * LAG

    @pl.loop(0, steps)
    def _(step):
        if AHEAD < units:
            @pl.when(step + AHEAD < units)
            def _():
                remote(0, step + AHEAD).start()
        for section in range(sections):
            unit = step - section * LAG

            @pl.when((unit >= 0) & (unit < units))
            def _():
                forward(section, unit)
        for i in range(per_step):
            @pl.when(step * per_step + i < boxes)
            def _():
                transpose_blocks(step * per_step + i)
        done = step - last + 1
        part = done // per_part

        @pl.when((done > 0) & (done <= units) & (done == part * per_part))
        def _():
            traces(part - 1)
        for section in range(sections - 1, 0, -1):
            unit = step - turn - (sections - 1 - section) * LAG

            @pl.when((unit >= 0) & (unit < units))
            def _():
                adjoint(section, unit)

    final = []
    for step in range(n_src):
        if step:
            final.append(pltpu.make_async_remote_copy(
                src_ref=image, dst_ref=arrived.at[0, step], send_sem=fin_send.at[0, step], recv_sem=fin_recv.at[0, step],
                device_id=(me_box, (me_src + step) % n_src), device_id_type=MESH))
        final.append(pltpu.make_async_remote_copy(
            src_ref=image_cross, dst_ref=arrived.at[1, step], send_sem=fin_send.at[1, step], recv_sem=fin_recv.at[1, step],
            device_id=(far, (me_src + step) % n_src), device_id_type=MESH))
    for copy in final:
        copy.start()

    refl_copy.wait_send()

    @pl.loop(0, units)
    def _(unit):
        for kind in range(2 * sections - 1):
            remote(kind, unit).wait_send()

    for copy in final:
        copy.wait()
    total = image[...] + arrived[1, 0]
    for step in range(1, n_src):
        total += arrived[0, step] + arrived[1, step]
    share = nodes // n_src
    for k in range(n_src):
        @pl.when(me_src == k)
        def _():
            out_ref[...] = total[:, k * share:(k + 1) * share]


def body(n_box, n_src, incident, reflectivity, w_self, w_cross, receivers, observed, group_of, deltas):
    boxes, sources, width = incident.shape
    nodes = width // 2
    sections = w_self.shape[0]
    units = PARTS * (boxes // GROUP)
    wave = (boxes, sources, width)
    anywhere = pl.BlockSpec(memory_space=pl.ANY)
    scalars = pl.BlockSpec(memory_space=pltpu.SMEM)
    vector = pl.BlockSpec(memory_space=pltpu.VMEM)
    bf16, f32 = jnp.bfloat16, jnp.float32
    return pl.pallas_call(
        functools.partial(kernel, n_box, n_src),
        out_shape=jax.ShapeDtypeStruct((boxes, nodes // n_src), f32),
        in_specs=[anywhere, anywhere, anywhere, anywhere, scalars, anywhere, vector, scalars],
        out_specs=vector,
        scratch_shapes=[
            pltpu.VMEM(wave, bf16),
            pltpu.VMEM(wave, bf16),
            pltpu.VMEM((boxes, nodes), f32),
            pltpu.VMEM((boxes, nodes), f32),
            pltpu.VMEM(w_self.shape, bf16),
            pltpu.VMEM(w_cross.shape, bf16),
            pltpu.VMEM(observed.shape, bf16),
            pltpu.VMEM((sections, boxes, width, width), bf16),
            pltpu.VMEM((sections, boxes, width, width), bf16),
            pltpu.VMEM((sections, boxes, width, width), bf16),
            pltpu.VMEM((sections, boxes, width, width), bf16),
            pltpu.VMEM((sections,) + wave, bf16),
            pltpu.VMEM((sections - 1,) + wave, bf16),
            pltpu.VMEM((sources, nodes), f32),
            pltpu.VMEM((receivers.shape[0], sources // PARTS, width), bf16),
            pltpu.VMEM((sections,) + wave, bf16),
            pltpu.VMEM((sections - 1,) + wave, bf16),
            pltpu.VMEM((sections - 1,) + wave, bf16),
            pltpu.VMEM((boxes, nodes), f32),
            pltpu.VMEM((boxes, nodes), f32),
            pltpu.VMEM((2, n_src, boxes, nodes), f32),
            pltpu.SemaphoreType.DMA((5,)),
            pltpu.SemaphoreType.DMA((2 * sections - 1, units)),
            pltpu.SemaphoreType.DMA((2 * sections - 1, units)),
            pltpu.SemaphoreType.DMA((2,)),
            pltpu.SemaphoreType.DMA((2, n_src)),
            pltpu.SemaphoreType.DMA((2, n_src)),
        ],
        compiler_params=pltpu.CompilerParams(
            collective_id=0, has_side_effects=True, vmem_limit_bytes=56 * 1024 * 1024),
    )(incident, reflectivity, w_self, w_cross, receivers, observed, group_of, deltas)


def solution(mesh):
    in_specs = (
        P("box", "src", None),
        P("box", None),
        P(None, "box", None, None, None),
        P(None, "box", None, None, None),
        P("box"),
        P("box", "src", None),
        P("src"),
        P(),
    )
    run = functools.partial(body, mesh.shape["box"], mesh.shape["src"])
    return jax.shard_map(run, mesh=mesh, in_specs=in_specs, out_specs=P("box", "src"), check_vma=False)
```
